128 devices in a mesh: node: 8 (over z, core), local: 16 (over y, x).
Axes of the slice: x: 4, y: 4, z: 4, core: 2. Of those that a mesh axis runs over, the one named last changes fastest.
Arguments:
- tokens: bfloat16 [2048, 3584], P(('node', 'local')), may hold values from -6 to 6
- expert_ids: int32 [2048, 8], P(('node', 'local')), may hold values from 0 to 127, as said below
- gate_values: bfloat16 [2048, 8], P(('node', 'local')), may hold values from 0.099609375 to 0.59765625
- w_gate: bfloat16 [128, 3584, 1024], P(('node', 'local')), may hold values from -0.09375 to 0.09375
- w_up: bfloat16 [128, 3584, 1024], P(('node', 'local')), may hold values from -0.09375 to 0.09375
- w_down: bfloat16 [128, 1024, 3584], P(('node', 'local')), may hold values from -0.1875 to 0.1875
Outputs:
- mixed: bfloat16 [2048, 3584], P(('node', 'local'))
The draws below stay inside these ranges and needn't reach their ends.
Inputs may be any that keep to these rules, and one draw needn't show every extreme that they name: `expert_ids`: A token's experts are distinct and lie in at most 4 groups, group g holding experts g * 16 to (g + 1) * 16 - 1. Among the 16 tokens of one device (aligned blocks of rows) no expert is named by more than 2 tokens, and in every draw some experts are named by exactly 2 tokens of every device.
All inputs are finite; a program needn't handle non-finite values.
Results may differ from the reference program's by a relative error of at most 0.0059.
Values may be sent and summed in bfloat16 or wider, within the bound.
No kernel may reach another device: no remote copies, remote signals or barrier semaphores. Data moves between devices by JAX's collectives and lax.ppermute only.
A program may use at most 64 MiB of HBM per device.

```python
import jax
import jax.numpy as jnp
from jax import lax

D = 3584
HID = 1024
TOPK = 8
NODE_LIMIT = 4
TOK_DEV = 16
PAIR = 2
NODES = 8
PER_NODE = 16
EXPERTS = 128
TOKENS = 2048


def draw_expert_ids(key, part):
    blocks = NODES * PER_NODE
    key_hot, key_noise, key_perm = jax.random.split(jax.random.fold_in(key, 11), 3)
    hot_node = jax.random.randint(key_hot, (), 0, NODES)
    noise = jax.random.randint(key_noise, (blocks, TOK_DEV, NODES), 0, 1 << 20)
    node_range = jnp.arange(NODES, dtype=jnp.int32)
    score = noise * NODES + node_range
    score = jnp.where(node_range == hot_node, 1 << 30, score)
    unused, chosen = lax.top_k(score, NODE_LIMIT)
    member = jnp.sum((chosen[..., None] == node_range).astype(jnp.int32), axis=2)
    before = jnp.cumsum(member, axis=1) - member
    rank = jnp.take_along_axis(before, chosen, axis=2)
    perm_keys = jax.random.split(key_perm, blocks * NODES)
    perms = jax.vmap(lambda single: jax.random.permutation(single, PER_NODE))(perm_keys).reshape(blocks, NODES, PER_NODE)
    chosen_perm = perms[jnp.arange(blocks)[:, None, None], chosen]
    within = (PAIR * rank[..., None] + jnp.arange(PAIR, dtype=jnp.int32)) % PER_NODE
    local_ids = jnp.take_along_axis(chosen_perm, within, axis=3)
    experts = chosen[..., None] * PER_NODE + local_ids
    return experts.reshape(TOKENS, TOPK).astype(jnp.int32)


def shard_levels(stream_key, extent, shards, smallest, top_value):
    level = 1.0
    for position, shards_of in shards:
        steps = jax.random.uniform(jax.random.fold_in(jax.random.fold_in(stream_key, 6), position), (shards_of,), jnp.float32, smallest / len(shards), top_value / len(shards))
        level = level * jnp.repeat(jnp.exp(steps), extent[position] // shards_of).reshape((-1,) + (1,) * (len(extent) - 1 - position))
    return level


def bell_draw(own_key, extent, scale, reach, cuts=(), held_as=jnp.bfloat16):
    entries = scale * jax.random.normal(own_key, extent, jnp.float32)
    if cuts:
        entries = entries * shard_levels(own_key, extent, cuts, -0.22, 0.18)
    return jnp.clip(entries, -reach, reach).astype(held_as)


def setup_inputs(seed: int = 0) -> dict:
    arg_keys = jax.random.split(jax.random.key(seed), 7)
    return {
        "tokens": bell_draw(arg_keys[0], (TOKENS, D), 1.0, 6.0, ((0, 128),)),
        "expert_ids": draw_expert_ids(jax.random.fold_in(arg_keys[6], 71), 0),
        "gate_values": jnp.clip(0.099609375 + 0.49804688 * jax.random.uniform(arg_keys[2], (TOKENS, TOPK), jnp.float32) ** shard_levels(arg_keys[2], (TOKENS, TOPK), ((0, 128),), -0.2, 0.2), 0.099609375, 0.59765625).astype(jnp.bfloat16),
        "w_gate": bell_draw(arg_keys[3], (EXPERTS, D, HID), D ** -0.5, 0.09375, ((0, 128),)),
        "w_up": bell_draw(arg_keys[4], (EXPERTS, D, HID), D ** -0.5, 0.09375, ((0, 128),)),
        "w_down": bell_draw(arg_keys[5], (EXPERTS, HID, D), HID ** -0.5, 0.1875, ((0, 128),)),
    }


def expert_rows(rows, gate_matrix, up_matrix, down_matrix):
    gate = jnp.dot(rows, gate_matrix, preferred_element_type=jnp.float32)
    upper = jnp.dot(rows, up_matrix, preferred_element_type=jnp.float32)
    hidden = (jax.nn.silu(gate) * upper).astype(jnp.bfloat16)
    return jnp.dot(hidden, down_matrix, preferred_element_type=jnp.float32).astype(jnp.bfloat16)


def reference(tokens, expert_ids, gate_values, w_gate, w_up, w_down):
    block = 64
    flat_ids = expert_ids.reshape(-1).astype(jnp.int32)
    count_all = flat_ids.shape[0]
    order = jnp.argsort(flat_ids, stable=True).astype(jnp.int32)
    counts = jnp.sum((flat_ids[:, None] == jnp.arange(EXPERTS, dtype=jnp.int32)[None, :]).astype(jnp.int32), axis=0)
    padded = ((counts + block - 1) // block) * block
    offsets = jnp.cumsum(padded) - padded
    starts = jnp.cumsum(counts) - counts
    sorted_ids = flat_ids[order]
    rank = jnp.arange(count_all, dtype=jnp.int32) - starts[sorted_ids]
    place = jnp.zeros((count_all,), jnp.int32).at[order].set((offsets[sorted_ids] + rank).astype(jnp.int32))
    blocks = count_all // block + EXPERTS
    total_rows = blocks * block
    token_of = (jnp.arange(count_all, dtype=jnp.int32) // TOPK).astype(jnp.int32)
    source = jnp.full((total_rows,), -1, jnp.int32).at[place].set(token_of)
    ends = offsets + padded
    block_starts = jnp.arange(blocks, dtype=jnp.int32) * block
    block_expert = jnp.minimum(jnp.sum((ends[None, :] <= block_starts[:, None]).astype(jnp.int32), axis=1), EXPERTS - 1).astype(jnp.int32)

    def run(index):
        picks = lax.dynamic_slice(source, (index * block,), (block,))
        expert = block_expert[index]
        rows = jnp.where((picks >= 0)[:, None], tokens[jnp.maximum(picks, 0)], jnp.zeros((), tokens.dtype))
        return expert_rows(rows, w_gate[expert], w_up[expert], w_down[expert])

    outputs = lax.map(run, jnp.arange(blocks, dtype=jnp.int32)).reshape(total_rows, D)
    picked = outputs[place].reshape(TOKENS, TOPK, D)
    total = jnp.sum(gate_values.astype(jnp.float32)[:, :, None] * picked.astype(jnp.float32), axis=1)
    return total.astype(jnp.bfloat16)
```

```python
import jax
import jax.numpy as jnp
from jax import lax
from jax.experimental import pallas as pl
from jax.experimental.pallas import tpu as pltpu
from jax.sharding import PartitionSpec as P

PAIR = 2
SEGMENTS = 4
BLOCK = PAIR * SEGMENTS
GROUP = 256

MIB = 1 << 20


def routing(ids_t, rows):
    topk, tok_count = ids_t.shape
    experts = rows // BLOCK
    expert = lax.broadcasted_iota(jnp.int32, (experts, tok_count), 0)
    used = jnp.zeros((experts, tok_count), jnp.float32)
    for k in range(topk):
        used = jnp.where(ids_t[k : k + 1, :] == expert, 1.0, used)
    wide = (tok_count, SEGMENTS * tok_count)
    column = lax.broadcasted_iota(jnp.int32, wide, 1) & (tok_count - 1)
    token = lax.broadcasted_iota(jnp.int32, wide, 0)
    weight = jnp.where(token < column, 1.0, jnp.where(token == column, -64.0, 0.0))
    rank = jnp.dot(used.astype(jnp.bfloat16), weight.astype(jnp.bfloat16), preferred_element_type=jnp.float32)
    rank = (rank + 64.0).astype(jnp.int32)
    shape = (experts, BLOCK, SEGMENTS * tok_count)
    rank = jnp.broadcast_to(rank[:, None, :], shape).reshape(rows, SEGMENTS * tok_count)
    row = lax.broadcasted_iota(jnp.int32, rank.shape, 0)
    lane = lax.broadcasted_iota(jnp.int32, rank.shape, 1)
    slot = row & (PAIR - 1)
    segment = (row & (BLOCK - 1)) >> 1
    return (rank == slot) & ((lane >> 4) == segment)


def dispatch_kernel(ids_ref, tokens_ref, out_ref):
    rows, width = out_ref.shape
    chosen = routing(ids_ref[...], rows)
    chosen = jnp.where(chosen, 1.0, 0.0).astype(jnp.bfloat16)
    table = jnp.concatenate(
        [tokens_ref[:, s * width : (s + 1) * width] for s in range(SEGMENTS)], axis=0
    )
    out_ref[...] = jnp.dot(chosen, table, preferred_element_type=jnp.float32).astype(jnp.bfloat16)


def weights_kernel(ids_ref, gates_ref, out_ref):
    rows = out_ref.shape[0]
    ids_t = ids_ref[...]
    topk, tok_count = ids_t.shape
    gates_t = gates_ref[...].astype(jnp.float32)
    experts = rows // BLOCK
    expert = lax.broadcasted_iota(jnp.int32, (experts, tok_count), 0)
    gate = jnp.zeros((experts, tok_count), jnp.float32)
    for k in range(topk):
        gate = jnp.where(ids_t[k : k + 1, :] == expert, gates_t[k : k + 1, :], gate)
    gate = jnp.concatenate([gate] * SEGMENTS, axis=1)
    shape = (experts, BLOCK, SEGMENTS * tok_count)
    gate = jnp.broadcast_to(gate[:, None, :], shape).reshape(rows, SEGMENTS * tok_count)
    out_ref[...] = jnp.where(routing(ids_t, rows), gate, 0.0).astype(jnp.bfloat16)


def combine_kernel(weights_ref, rows_ref, out_ref):
    tok_count = out_ref.shape[0]
    width = rows_ref.shape[1]
    total = lax.dot_general(
        weights_ref[...],
        rows_ref[...],
        (((0,), (0,)), ((), ())),
        preferred_element_type=jnp.float32,
    ).astype(jnp.bfloat16)
    for s in range(SEGMENTS):
        out_ref[:, s * width : (s + 1) * width] = total[s * tok_count : (s + 1) * tok_count, :]


def reorder(forward):
    part = GROUP // SEGMENTS
    a = lax.broadcasted_iota(jnp.int32, (GROUP, GROUP), 0 if forward else 1)
    b = lax.broadcasted_iota(jnp.int32, (GROUP, GROUP), 1 if forward else 0)
    inside = a & (part - 1)
    place = (inside >> 1) * BLOCK + (a >> 6) * PAIR + (inside & 1)
    return jnp.where(place == b, 1.0, 0.0).astype(jnp.bfloat16)


def expert_kernel(rows_ref, gate_ref, up_ref, down_ref, out_ref, x_ref, h_ref, y_ref):
    total, width = rows_ref.shape
    part = GROUP // SEGMENTS
    groups = total // GROUP
    hid = gate_ref.shape[1]
    depth = down_ref.shape[1]
    forward = reorder(True)
    for g in range(groups):
        block = jnp.dot(
            forward, rows_ref[g * GROUP : (g + 1) * GROUP, :], preferred_element_type=jnp.float32
        ).astype(jnp.bfloat16)
        for s in range(SEGMENTS):
            x_ref[g * part : (g + 1) * part, s * width : (s + 1) * width] = block[
                s * part : (s + 1) * part, :
            ]
    tile = 256

    @pl.loop(0, hid // tile)
    def _(n):
        columns = pl.ds(pl.multiple_of(n * tile, tile), tile)
        gate = jnp.dot(x_ref[...], gate_ref[:, columns], preferred_element_type=jnp.float32)
        upper = jnp.dot(x_ref[...], up_ref[:, columns], preferred_element_type=jnp.float32)
        h_ref[:, columns] = (gate / (1.0 + jnp.exp(-gate)) * upper).astype(jnp.bfloat16)

    wide = 512

    @pl.loop(0, depth // wide)
    def _(n):
        columns = pl.ds(pl.multiple_of(n * wide, wide), wide)
        y_ref[:, columns] = jnp.dot(
            h_ref[...], down_ref[:, columns], preferred_element_type=jnp.float32
        ).astype(jnp.bfloat16)

    back = reorder(False)
    for g in range(groups):
        block = jnp.concatenate(
            [
                y_ref[g * part : (g + 1) * part, s * width : (s + 1) * width]
                for s in range(SEGMENTS)
            ],
            axis=0,
        )
        out_ref[g * GROUP : (g + 1) * GROUP, :] = jnp.dot(
            back, block, preferred_element_type=jnp.float32
        ).astype(jnp.bfloat16)


def vmem():
    return pl.BlockSpec(memory_space=pltpu.VMEM)


def call(kernel, out_shape, inputs, limit, scratch=(), flops=0, moved=0):
    return pl.pallas_call(
        kernel,
        out_shape=out_shape,
        in_specs=[vmem()] * inputs,
        out_specs=vmem(),
        scratch_shapes=list(scratch),
        compiler_params=pltpu.CompilerParams(vmem_limit_bytes=limit),
        cost_estimate=pl.CostEstimate(flops=flops, bytes_accessed=moved, transcendentals=0),
    )


def local(tokens, expert_ids, gate_values, w_gate, w_up, w_down):
    tok_count, width = tokens.shape
    hid = w_gate.shape[2]
    experts = lax.axis_size("node") * lax.axis_size("local")
    rows = experts * BLOCK
    piece = width // SEGMENTS
    bf16 = jnp.bfloat16
    ids_t = expert_ids.T
    gates_t = gate_values.T
    outgoing = call(
        dispatch_kernel, jax.ShapeDtypeStruct((rows, piece), bf16), 2, 12 * MIB,
        flops=2 * rows * 64 * piece, moved=2 * rows * piece,
    )(ids_t, tokens)
    weights = call(
        weights_kernel, jax.ShapeDtypeStruct((rows, SEGMENTS * tok_count), bf16), 2, 8 * MIB,
        moved=2 * rows * 64,
    )(ids_t, gates_t)
    incoming = lax.all_to_all(
        outgoing.reshape(experts, BLOCK, piece), ("node", "local"), split_axis=0, concat_axis=0, tiled=True
    )
    m = experts * PAIR
    result = call(
        expert_kernel, jax.ShapeDtypeStruct((rows, piece), bf16), 4, 16 * MIB,
        scratch=(
            pltpu.VMEM((m, width), bf16),
            pltpu.VMEM((m, hid), bf16),
            pltpu.VMEM((m, width), bf16),
        ),
        flops=6 * m * width * hid, moved=6 * width * hid,
    )(incoming.reshape(rows, piece), w_gate[0], w_up[0], w_down[0])
    answered = lax.all_to_all(
        result.reshape(experts, BLOCK, piece), ("node", "local"), split_axis=0, concat_axis=0, tiled=True
    )
    return call(
        combine_kernel, jax.ShapeDtypeStruct((tok_count, width), bf16), 2, 12 * MIB,
        flops=2 * rows * 64 * piece, moved=2 * rows * piece,
    )(weights, answered.reshape(rows, piece))


def solution(mesh):
    return jax.shard_map(
        local,
        mesh=mesh,
        in_specs=(
            P(("node", "local"), None),
            P(("node", "local"), None),
            P(("node", "local"), None),
            P(("node", "local"), None, None),
            P(("node", "local"), None, None),
            P(("node", "local"), None, None),
        ),
        out_specs=P(("node", "local"), None),
        check_vma=False,
    )
```

```python
import jax
import jax.numpy as jnp
from jax import lax
from jax.experimental import pallas as pl
from jax.experimental.pallas import tpu as pltpu
from jax.sharding import PartitionSpec as P

PAIR = 2
SEGMENTS = 4
BLOCK = PAIR * SEGMENTS
GROUP = 256

MIB = 1 << 20


def routing(ids_t, rows):
    topk, tok_count = ids_t.shape
    experts = rows // BLOCK
    expert = lax.broadcasted_iota(jnp.int32, (experts, tok_count), 0)
    used = jnp.zeros((experts, tok_count), jnp.float32)
    for k in range(topk):
        used = jnp.where(ids_t[k : k + 1, :] == expert, 1.0, used)
    wide = (tok_count, SEGMENTS * tok_count)
    column = lax.broadcasted_iota(jnp.int32, wide, 1) & (tok_count - 1)
    token = lax.broadcasted_iota(jnp.int32, wide, 0)
    weight = jnp.where(token < column, 1.0, jnp.where(token == column, -64.0, 0.0))
    rank = jnp.dot(used.astype(jnp.bfloat16), weight.astype(jnp.bfloat16), preferred_element_type=jnp.float32)
    rank = (rank + 64.0).astype(jnp.int32)
    shape = (experts, BLOCK, SEGMENTS * tok_count)
    rank = jnp.broadcast_to(rank[:, None, :], shape).reshape(rows, SEGMENTS * tok_count)
    row = lax.broadcasted_iota(jnp.int32, rank.shape, 0)
    lane = lax.broadcasted_iota(jnp.int32, rank.shape, 1)
    slot = row & (PAIR - 1)
    segment = (row & (BLOCK - 1)) >> 1
    return (rank == slot) & ((lane >> 4) == segment)


def dispatch_kernel(ids_ref, tokens_ref, out_ref):
    rows, width = out_ref.shape
    chosen = routing(ids_ref[...], rows)
    chosen = jnp.where(chosen, 1.0, 0.0).astype(jnp.bfloat16)
    table = jnp.concatenate(
        [tokens_ref[:, s * width : (s + 1) * width] for s in range(SEGMENTS)], axis=0
    )
    out_ref[...] = jnp.dot(chosen, table, preferred_element_type=jnp.float32).astype(jnp.bfloat16)


def weights_kernel(ids_ref, gates_ref, out_ref):
    rows = out_ref.shape[0]
    ids_t = ids_ref[...]
    topk, tok_count = ids_t.shape
    gates_t = gates_ref[...].astype(jnp.float32)
    experts = rows // BLOCK
    expert = lax.broadcasted_iota(jnp.int32, (experts, tok_count), 0)
    gate = jnp.zeros((experts, tok_count), jnp.float32)
    for k in range(topk):
        gate = jnp.where(ids_t[k : k + 1, :] == expert, gates_t[k : k + 1, :], gate)
    gate = jnp.concatenate([gate] * SEGMENTS, axis=1)
    shape = (experts, BLOCK, SEGMENTS * tok_count)
    gate = jnp.broadcast_to(gate[:, None, :], shape).reshape(rows, SEGMENTS * tok_count)
    out_ref[...] = jnp.where(routing(ids_t, rows), gate, 0.0).astype(jnp.bfloat16)


def combine_kernel(weights_ref, rows_ref, out_ref):
    tok_count = out_ref.shape[0]
    width = rows_ref.shape[1]
    total = lax.dot_general(
        weights_ref[...],
        rows_ref[...],
        (((0,), (0,)), ((), ())),
        preferred_element_type=jnp.float32,
    ).astype(jnp.bfloat16)
    for s in range(SEGMENTS):
        out_ref[:, s * width : (s + 1) * width] = total[s * tok_count : (s + 1) * tok_count, :]


def reorder(forward):
    part = GROUP // SEGMENTS
    a = lax.broadcasted_iota(jnp.int32, (GROUP, GROUP), 0 if forward else 1)
    b = lax.broadcasted_iota(jnp.int32, (GROUP, GROUP), 1 if forward else 0)
    inside = a & (part - 1)
    place = (inside >> 1) * BLOCK + (a >> 6) * PAIR + (inside & 1)
    return jnp.where(place == b, 1.0, 0.0).astype(jnp.bfloat16)


def expert_kernel(rows_ref, gate_ref, up_ref, down_ref, out_ref, x_ref, h_ref, y_ref):
    total, width = rows_ref.shape
    part = GROUP // SEGMENTS
    groups = total // GROUP
    hid = gate_ref.shape[1]
    depth = down_ref.shape[1]
    forward = reorder(True)
    for g in range(groups):
        block = jnp.dot(
            forward, rows_ref[g * GROUP : (g + 1) * GROUP, :], preferred_element_type=jnp.float32
        ).astype(jnp.bfloat16)
        for s in range(SEGMENTS):
            x_ref[g * part : (g + 1) * part, s * width : (s + 1) * width] = block[
                s * part : (s + 1) * part, :
            ]
    tile = 256

    @pl.loop(0, hid // tile)
    def _(n):
        columns = pl.ds(pl.multiple_of(n * tile, tile), tile)
        gate = jnp.dot(x_ref[...], gate_ref[:, columns], preferred_element_type=jnp.float32)
        upper = jnp.dot(x_ref[...], up_ref[:, columns], preferred_element_type=jnp.float32)
        h_ref[:, columns] = (gate / (1.0 + jnp.exp(-gate)) * upper).astype(jnp.bfloat16)

    wide = 512

    @pl.loop(0, depth // wide)
    def _(n):
        columns = pl.ds(pl.multiple_of(n * wide, wide), wide)
        y_ref[:, columns] = jnp.dot(
            h_ref[...], down_ref[:, columns], preferred_element_type=jnp.float32
        ).astype(jnp.bfloat16)

    back = reorder(False)
    for g in range(groups):
        block = jnp.concatenate(
            [
                y_ref[g * part : (g + 1) * part, s * width : (s + 1) * width]
                for s in range(SEGMENTS)
            ],
            axis=0,
        )
        out_ref[g * GROUP : (g + 1) * GROUP, :] = jnp.dot(
            back, block, preferred_element_type=jnp.float32
        ).astype(jnp.bfloat16)


def vmem():
    return pl.BlockSpec(memory_space=pltpu.VMEM)


def call(kernel, out_shape, inputs, limit, scratch=(), flops=0, moved=0):
    return pl.pallas_call(
        kernel,
        out_shape=out_shape,
        in_specs=[vmem()] * inputs,
        out_specs=vmem(),
        scratch_shapes=list(scratch),
        compiler_params=pltpu.CompilerParams(vmem_limit_bytes=limit),
        cost_estimate=pl.CostEstimate(flops=flops, bytes_accessed=moved, transcendentals=0),
    )


def local(tokens, expert_ids, gate_values, w_gate, w_up, w_down):
    tok_count, width = tokens.shape
    hid = w_gate.shape[2]
    experts = lax.axis_size("node") * lax.axis_size("local")
    rows = experts * BLOCK
    piece = width // SEGMENTS
    bf16 = jnp.bfloat16
    ids_t = expert_ids.T
    gates_t = gate_values.T
    outgoing = call(
        dispatch_kernel, jax.ShapeDtypeStruct((rows, piece), bf16), 2, 12 * MIB,
        flops=30_000_000_000, moved=60_000_000,
    )(ids_t, tokens)
    weights = call(
        weights_kernel, jax.ShapeDtypeStruct((rows, SEGMENTS * tok_count), bf16), 2, 8 * MIB,
        moved=2 * rows * 64,
    )(ids_t, gates_t)
    incoming = lax.all_to_all(
        outgoing.reshape(experts, BLOCK, piece), ("node", "local"), split_axis=0, concat_axis=0, tiled=True
    )
    m = experts * PAIR
    result = call(
        expert_kernel, jax.ShapeDtypeStruct((rows, piece), bf16), 4, 16 * MIB,
        scratch=(
            pltpu.VMEM((m, width), bf16),
            pltpu.VMEM((m, hid), bf16),
            pltpu.VMEM((m, width), bf16),
        ),
        flops=6 * m * width * hid, moved=6 * width * hid,
    )(incoming.reshape(rows, piece), w_gate[0], w_up[0], w_down[0])
    answered = lax.all_to_all(
        result.reshape(experts, BLOCK, piece), ("node", "local"), split_axis=0, concat_axis=0, tiled=True
    )
    return call(
        combine_kernel, jax.ShapeDtypeStruct((tok_count, width), bf16), 2, 12 * MIB,
        flops=2 * rows * 64 * piece, moved=2 * rows * piece,
    )(weights, answered.reshape(rows, piece))


def solution(mesh):
    return jax.shard_map(
        local,
        mesh=mesh,
        in_specs=(
            P(("node", "local"), None),
            P(("node", "local"), None),
            P(("node", "local"), None),
            P(("node", "local"), None, None),
            P(("node", "local"), None, None),
            P(("node", "local"), None, None),
        ),
        out_specs=P(("node", "local"), None),
        check_vma=False,
    )
```

```python
import jax
import jax.numpy as jnp
from jax import lax
from jax.experimental import pallas as pl
from jax.experimental.pallas import tpu as pltpu
from jax.sharding import PartitionSpec as P

PAIR = 2
SEGMENTS = 4
BLOCK = PAIR * SEGMENTS
GROUP = 256

MIB = 1 << 20


def routing(ids_t, rows):
    topk, tok_count = ids_t.shape
    experts = rows // BLOCK
    expert = lax.broadcasted_iota(jnp.int32, (experts, tok_count), 0)
    used = jnp.zeros((experts, tok_count), jnp.float32)
    for k in range(topk):
        used = jnp.where(ids_t[k : k + 1, :] == expert, 1.0, used)
    wide = (tok_count, SEGMENTS * tok_count)
    column = lax.broadcasted_iota(jnp.int32, wide, 1) & (tok_count - 1)
    token = lax.broadcasted_iota(jnp.int32, wide, 0)
    weight = jnp.where(token < column, 1.0, jnp.where(token == column, -64.0, 0.0))
    rank = jnp.dot(used.astype(jnp.bfloat16), weight.astype(jnp.bfloat16), preferred_element_type=jnp.float32)
    rank = (rank + 64.0).astype(jnp.int32)
    shape = (experts, BLOCK, SEGMENTS * tok_count)
    rank = jnp.broadcast_to(rank[:, None, :], shape).reshape(rows, SEGMENTS * tok_count)
    row = lax.broadcasted_iota(jnp.int32, rank.shape, 0)
    lane = lax.broadcasted_iota(jnp.int32, rank.shape, 1)
    slot = row & (PAIR - 1)
    segment = (row & (BLOCK - 1)) >> 1
    return (rank == slot) & ((lane >> 4) == segment)


def dispatch_kernel(ids_hbm, tokens_hbm, out_ref, ids_ref, tokens_ref, sems):
    ids_copy = pltpu.make_async_copy(ids_hbm, ids_ref, sems.at[0])
    tokens_copy = pltpu.make_async_copy(tokens_hbm, tokens_ref, sems.at[1])
    ids_copy.start()
    tokens_copy.start()
    rows, width = out_ref.shape
    ids_copy.wait()
    chosen = routing(ids_ref[...], rows)
    chosen = jnp.where(chosen, 1.0, 0.0).astype(jnp.bfloat16)
    tokens_copy.wait()
    table = jnp.concatenate(
        [tokens_ref[:, s * width : (s + 1) * width] for s in range(SEGMENTS)], axis=0
    )
    out_ref[...] = jnp.dot(chosen, table, preferred_element_type=jnp.float32).astype(jnp.bfloat16)


def gate_table(ids_t, gates_t, rows):
    topk, tok_count = ids_t.shape
    experts = rows // BLOCK
    expert = lax.broadcasted_iota(jnp.int32, (experts, tok_count), 0)
    gate = jnp.zeros((experts, tok_count), jnp.float32)
    for k in range(topk):
        gate = jnp.where(ids_t[k : k + 1, :] == expert, gates_t[k : k + 1, :], gate)
    gate = jnp.concatenate([gate] * SEGMENTS, axis=1)
    shape = (experts, BLOCK, SEGMENTS * tok_count)
    gate = jnp.broadcast_to(gate[:, None, :], shape).reshape(rows, SEGMENTS * tok_count)
    return jnp.where(routing(ids_t, rows), gate, 0.0).T.astype(jnp.bfloat16)


def combine_kernel(weights_ref, rows_ref, out_ref):
    tok_count = out_ref.shape[0]
    width = rows_ref.shape[1]
    total = jnp.dot(weights_ref[...], rows_ref[...], preferred_element_type=jnp.float32)
    total = total.astype(jnp.bfloat16)
    for s in range(SEGMENTS):
        out_ref[:, s * width : (s + 1) * width] = total[s * tok_count : (s + 1) * tok_count, :]


def reorder(forward):
    part = GROUP // SEGMENTS
    a = lax.broadcasted_iota(jnp.int32, (GROUP, GROUP), 0 if forward else 1)
    b = lax.broadcasted_iota(jnp.int32, (GROUP, GROUP), 1 if forward else 0)
    inside = a & (part - 1)
    place = (inside >> 1) * BLOCK + (a >> 6) * PAIR + (inside & 1)
    return jnp.where(place == b, 1.0, 0.0).astype(jnp.bfloat16)


def expert_kernel(
    rows_ref, gate_ref, up_ref, down_ref, ids_ref, gates_ref, out_ref, weights_ref, x_ref, h_ref, y_ref
):
    total, width = rows_ref.shape
    part = GROUP // SEGMENTS
    groups = total // GROUP
    hid = gate_ref.shape[1]
    depth = down_ref.shape[1]
    tile = 512
    forward = reorder(True)
    for g in range(groups):
        block = jnp.dot(
            forward, rows_ref[g * GROUP : (g + 1) * GROUP, :], preferred_element_type=jnp.float32
        ).astype(jnp.bfloat16)
        for s in range(SEGMENTS):
            x_ref[g * part : (g + 1) * part, s * width : (s + 1) * width] = block[
                s * part : (s + 1) * part, :
            ]
    for n in range(hid // tile):
        columns = slice(n * tile, (n + 1) * tile)
        gate = jnp.dot(x_ref[...], gate_ref[:, columns], preferred_element_type=jnp.float32)
        upper = jnp.dot(x_ref[...], up_ref[:, columns], preferred_element_type=jnp.float32)
        h_ref[:, columns] = (gate / (1.0 + jnp.exp(-gate)) * upper).astype(jnp.bfloat16)
    weights_ref[...] = gate_table(ids_ref[...], gates_ref[...].astype(jnp.float32), total)
    for n in range(depth // tile):
        columns = slice(n * tile, (n + 1) * tile)
        y_ref[:, columns] = jnp.dot(
            h_ref[...], down_ref[:, columns], preferred_element_type=jnp.float32
        ).astype(jnp.bfloat16)
    back = reorder(False)
    for g in range(groups):
        block = jnp.concatenate(
            [
                y_ref[g * part : (g + 1) * part, s * width : (s + 1) * width]
                for s in range(SEGMENTS)
            ],
            axis=0,
        )
        out_ref[g * GROUP : (g + 1) * GROUP, :] = jnp.dot(
            back, block, preferred_element_type=jnp.float32
        ).astype(jnp.bfloat16)


def exchange(rows, experts, piece):
    blocks = rows.reshape(experts, BLOCK, piece)
    moved = lax.all_to_all(blocks, ("node", "local"), split_axis=0, concat_axis=0, tiled=True)
    return moved.reshape(rows.shape)


def vmem():
    return pl.BlockSpec(memory_space=pltpu.VMEM)


def local(tokens, expert_ids, gate_values, w_gate, w_up, w_down):
    tok_count, width = tokens.shape
    topk = expert_ids.shape[1]
    hid = w_gate.shape[2]
    experts = lax.axis_size("node") * lax.axis_size("local")
    rows = experts * BLOCK
    piece = width // SEGMENTS
    m = experts * PAIR
    bf16 = jnp.bfloat16
    hbm = pl.BlockSpec(memory_space=pltpu.HBM)
    ids_t = expert_ids.T
    outgoing = pl.pallas_call(
        dispatch_kernel,
        out_shape=jax.ShapeDtypeStruct((rows, piece), bf16),
        in_specs=[hbm] * 2,
        out_specs=vmem(),
        scratch_shapes=[
            pltpu.VMEM((topk, tok_count), jnp.int32),
            pltpu.VMEM((tok_count, width), bf16),
            pltpu.SemaphoreType.DMA((2,)),
        ],
        compiler_params=pltpu.CompilerParams(vmem_limit_bytes=12 * MIB),
        cost_estimate=pl.CostEstimate(
            flops=30_000_000_000, bytes_accessed=60_000_000, transcendentals=0
        ),
    )(*(pltpu.with_memory_space_constraint(v, pltpu.HBM) for v in (ids_t, tokens)))
    incoming = exchange(outgoing, experts, piece)
    result, weights = pl.pallas_call(
        expert_kernel,
        out_shape=[
            jax.ShapeDtypeStruct((rows, piece), bf16),
            jax.ShapeDtypeStruct((SEGMENTS * tok_count, rows), bf16),
        ],
        in_specs=[vmem()] * 6,
        out_specs=[vmem()] * 2,
        scratch_shapes=[
            pltpu.VMEM((m, width), bf16),
            pltpu.VMEM((m, hid), bf16),
            pltpu.VMEM((m, width), bf16),
        ],
        compiler_params=pltpu.CompilerParams(vmem_limit_bytes=20 * MIB),
        cost_estimate=pl.CostEstimate(
            flops=6 * m * width * hid, bytes_accessed=6 * width * hid, transcendentals=m * hid
        ),
    )(incoming, w_gate[0], w_up[0], w_down[0], ids_t, gate_values.T)
    answered = exchange(result, experts, piece)
    return pl.pallas_call(
        combine_kernel,
        out_shape=jax.ShapeDtypeStruct((tok_count, width), bf16),
        in_specs=[vmem()] * 2,
        out_specs=vmem(),
        compiler_params=pltpu.CompilerParams(vmem_limit_bytes=12 * MIB),
        cost_estimate=pl.CostEstimate(
            flops=2 * rows * 64 * piece, bytes_accessed=2 * rows * piece, transcendentals=0
        ),
    )(weights, answered)


def solution(mesh):
    return jax.shard_map(
        local,
        mesh=mesh,
        in_specs=(
            P(("node", "local"), None),
            P(("node", "local"), None),
            P(("node", "local"), None),
            P(("node", "local"), None, None),
            P(("node", "local"), None, None),
            P(("node", "local"), None, None),
        ),
        out_specs=P(("node", "local"), None),
        check_vma=False,
    )
```

```python
import jax
import jax.numpy as jnp
from jax import lax
from jax.experimental import pallas as pl
from jax.experimental.pallas import tpu as pltpu
from jax.sharding import PartitionSpec as P

PAIR = 2
TILE = 512
MIB = 1 << 20


def routing(ids_t, rows):
    topk, tok_count = ids_t.shape
    row = lax.broadcasted_iota(jnp.int32, (rows, tok_count), 0)
    expert = row >> 1
    used = jnp.zeros((rows, tok_count), jnp.float32)
    for k in range(topk):
        used = jnp.where(ids_t[k : k + 1, :] == expert, 1.0, used)
    column = lax.broadcasted_iota(jnp.int32, (tok_count, tok_count), 1)
    token = lax.broadcasted_iota(jnp.int32, (tok_count, tok_count), 0)
    weight = jnp.where(token < column, 1.0, jnp.where(token == column, -64.0, 0.0))
    rank = jnp.dot(used.astype(jnp.bfloat16), weight.astype(jnp.bfloat16), preferred_element_type=jnp.float32)
    return expert, (rank + 64.0).astype(jnp.int32) == (row & (PAIR - 1))


def dispatch_kernel(ids_hbm, tokens_hbm, out_ref, ids_ref, tokens_ref, sems):
    ids_copy = pltpu.make_async_copy(ids_hbm, ids_ref, sems.at[0])
    tokens_copy = pltpu.make_async_copy(tokens_hbm, tokens_ref, sems.at[1])
    ids_copy.start()
    tokens_copy.start()
    experts, pair, width = out_ref.shape
    ids_copy.wait()
    _, chosen = routing(ids_ref[...], experts * pair)
    chosen = jnp.where(chosen, 1.0, 0.0).astype(jnp.bfloat16)
    tokens_copy.wait()
    for n in range(width // TILE):
        columns = slice(n * TILE, (n + 1) * TILE)
        block = jnp.dot(chosen, tokens_ref[:, columns], preferred_element_type=jnp.float32)
        out_ref[:, :, columns] = block.astype(jnp.bfloat16).reshape(experts, pair, TILE)


def gate_table(ids_t, gates_t, rows):
    expert, chosen = routing(ids_t, rows)
    gate = jnp.zeros(expert.shape, jnp.float32)
    for k in range(ids_t.shape[0]):
        gate = jnp.where(ids_t[k : k + 1, :] == expert, gates_t[k : k + 1, :], gate)
    return jnp.where(chosen, gate, 0.0).T.astype(jnp.bfloat16)


def expert_kernel(rows_ref, gate_ref, up_ref, down_ref, ids_ref, gates_ref, out_ref, table_ref, x_ref, h_ref):
    experts, pair, width = rows_ref.shape
    rows = experts * pair
    hid = gate_ref.shape[1]
    for n in range(width // TILE):
        columns = slice(n * TILE, (n + 1) * TILE)
        x_ref[:, columns] = rows_ref[:, :, columns].reshape(rows, TILE)
    for n in range(hid // TILE):
        columns = slice(n * TILE, (n + 1) * TILE)
        gate = jnp.dot(x_ref[...], gate_ref[:, columns], preferred_element_type=jnp.float32)
        upper = jnp.dot(x_ref[...], up_ref[:, columns], preferred_element_type=jnp.float32)
        h_ref[:, columns] = (gate / (1.0 + jnp.exp(-gate)) * upper).astype(jnp.bfloat16)
    table_ref[...] = gate_table(ids_ref[...], gates_ref[...].astype(jnp.float32), rows)
    for n in range(width // TILE):
        columns = slice(n * TILE, (n + 1) * TILE)
        block = jnp.dot(h_ref[...], down_ref[:, columns], preferred_element_type=jnp.float32)
        out_ref[:, :, columns] = block.astype(jnp.bfloat16).reshape(experts, pair, TILE)


def combine_kernel(table_ref, rows_ref, out_ref):
    experts, pair, width = rows_ref.shape
    for n in range(width // TILE):
        columns = slice(n * TILE, (n + 1) * TILE)
        block = rows_ref[:, :, columns].reshape(experts * pair, TILE)
        total = jnp.dot(table_ref[...], block, preferred_element_type=jnp.float32)
        out_ref[:, columns] = total.astype(jnp.bfloat16)


def exchange(blocks):
    return lax.all_to_all(blocks, ("node", "local"), split_axis=0, concat_axis=0, tiled=True)


def local(tokens, expert_ids, gate_values, w_gate, w_up, w_down):
    tok_count, width = tokens.shape
    topk = expert_ids.shape[1]
    hid = w_gate.shape[2]
    experts = lax.axis_size("node") * lax.axis_size("local")
    rows = experts * PAIR
    bf16 = jnp.bfloat16
    hbm = pl.BlockSpec(memory_space=pltpu.HBM)
    vmem = pl.BlockSpec(memory_space=pltpu.VMEM)
    ids_t = expert_ids.T
    outgoing = pl.pallas_call(
        dispatch_kernel,
        out_shape=jax.ShapeDtypeStruct((experts, PAIR, width), bf16),
        in_specs=[hbm] * 2,
        out_specs=vmem,
        scratch_shapes=[
            pltpu.VMEM((topk, tok_count), jnp.int32),
            pltpu.VMEM((tok_count, width), bf16),
            pltpu.SemaphoreType.DMA((2,)),
        ],
        compiler_params=pltpu.CompilerParams(vmem_limit_bytes=12 * MIB),
        cost_estimate=pl.CostEstimate(
            flops=30_000_000_000, bytes_accessed=60_000_000, transcendentals=0
        ),
    )(*(pltpu.with_memory_space_constraint(v, pltpu.HBM) for v in (ids_t, tokens)))
    incoming = exchange(outgoing)
    result, table = pl.pallas_call(
        expert_kernel,
        out_shape=[
            jax.ShapeDtypeStruct((experts, PAIR, width), bf16),
            jax.ShapeDtypeStruct((tok_count, rows), bf16),
        ],
        in_specs=[vmem] * 6,
        out_specs=[vmem] * 2,
        scratch_shapes=[pltpu.VMEM((rows, width), bf16), pltpu.VMEM((rows, hid), bf16)],
        compiler_params=pltpu.CompilerParams(vmem_limit_bytes=20 * MIB),
        cost_estimate=pl.CostEstimate(
            flops=6 * rows * width * hid, bytes_accessed=6 * width * hid, transcendentals=rows * hid
        ),
    )(incoming, w_gate[0], w_up[0], w_down[0], ids_t, gate_values.T)
    answered = exchange(result)
    return pl.pallas_call(
        combine_kernel,
        out_shape=jax.ShapeDtypeStruct((tok_count, width), bf16),
        in_specs=[vmem] * 2,
        out_specs=vmem,
        compiler_params=pltpu.CompilerParams(vmem_limit_bytes=12 * MIB),
        cost_estimate=pl.CostEstimate(
            flops=2 * rows * tok_count * width, bytes_accessed=2 * rows * width, transcendentals=0
        ),
    )(table, answered)


def solution(mesh):
    return jax.shard_map(
        local,
        mesh=mesh,
        in_specs=(
            P(("node", "local"), None),
            P(("node", "local"), None),
            P(("node", "local"), None),
            P(("node", "local"), None, None),
            P(("node", "local"), None, None),
            P(("node", "local"), None, None),
        ),
        out_specs=P(("node", "local"), None),
        check_vma=False,
    )
```

```python
import jax
import jax.numpy as jnp
from jax import lax
from jax.experimental import pallas as pl
from jax.experimental.pallas import tpu as pltpu
from jax.sharding import PartitionSpec as P

PAIR = 2
TILE = 512
MIB = 1 << 20


def routing(ids_t, rows):
    topk, tok_count = ids_t.shape
    row = lax.broadcasted_iota(jnp.int32, (rows, tok_count), 0)
    expert = row >> 1
    used = jnp.zeros((rows, tok_count), jnp.float32)
    for k in range(topk):
        used = jnp.where(ids_t[k : k + 1, :] == expert, 1.0, used)
    column = lax.broadcasted_iota(jnp.int32, (tok_count, tok_count), 1)
    token = lax.broadcasted_iota(jnp.int32, (tok_count, tok_count), 0)
    weight = jnp.where(token < column, 1.0, jnp.where(token == column, -64.0, 0.0))
    rank = jnp.dot(used.astype(jnp.bfloat16), weight.astype(jnp.bfloat16), preferred_element_type=jnp.float32)
    return (rank + 64.0).astype(jnp.int32) == (row & (PAIR - 1))


def dispatch_kernel(ids_hbm, tokens_hbm, out_ref, ids_ref, tokens_ref, sems):
    ids_copy = pltpu.make_async_copy(ids_hbm, ids_ref, sems.at[0])
    tokens_copy = pltpu.make_async_copy(tokens_hbm, tokens_ref, sems.at[1])
    ids_copy.start()
    tokens_copy.start()
    experts, pair, width = out_ref.shape
    ids_copy.wait()
    chosen = routing(ids_ref[...], experts * pair)
    chosen = jnp.where(chosen, 1.0, 0.0).astype(jnp.bfloat16)
    tokens_copy.wait()
    for n in range(width // TILE):
        columns = slice(n * TILE, (n + 1) * TILE)
        block = jnp.dot(chosen, tokens_ref[:, columns], preferred_element_type=jnp.float32)
        out_ref[:, :, columns] = block.astype(jnp.bfloat16).reshape(experts, pair, TILE)


def gate_table(ids_t, gates_t, rows):
    topk, tok_count = ids_t.shape
    ids = ids_t.astype(jnp.float32).T
    gates = gates_t.T
    column = lax.broadcasted_iota(jnp.int32, (tok_count, rows), 1)
    expert = (column >> 1).astype(jnp.float32)
    gate = jnp.zeros((tok_count, rows), jnp.float32)
    used = jnp.zeros((tok_count, rows), jnp.float32)
    for k in range(topk):
        hit = ids[:, k : k + 1] == expert
        gate = jnp.where(hit, gates[:, k : k + 1], gate)
        used = jnp.where(hit, 1.0, used)
    token = lax.broadcasted_iota(jnp.int32, (tok_count, tok_count), 0)
    other = lax.broadcasted_iota(jnp.int32, (tok_count, tok_count), 1)
    weight = jnp.where(other < token, 1.0, jnp.where(other == token, -64.0, 0.0))
    rank = jnp.dot(weight.astype(jnp.bfloat16), used.astype(jnp.bfloat16), preferred_element_type=jnp.float32)
    chosen = (rank + 64.0).astype(jnp.int32) == (column & (PAIR - 1))
    return jnp.where(chosen, gate, 0.0).astype(jnp.bfloat16)


def expert_kernel(rows_ref, gate_ref, up_ref, down_ref, ids_ref, gates_ref, out_ref, table_ref, x_ref, h_ref):
    experts, pair, width = rows_ref.shape
    rows = experts * pair
    hid = gate_ref.shape[1]
    for n in range(width // TILE):
        columns = slice(n * TILE, (n + 1) * TILE)
        x_ref[:, columns] = rows_ref[:, :, columns].reshape(rows, TILE)
    for n in range(hid // TILE):
        columns = slice(n * TILE, (n + 1) * TILE)
        gate = jnp.dot(x_ref[...], gate_ref[:, columns], preferred_element_type=jnp.float32)
        upper = jnp.dot(x_ref[...], up_ref[:, columns], preferred_element_type=jnp.float32)
        h_ref[:, columns] = (gate / (1.0 + jnp.exp(-gate)) * upper).astype(jnp.bfloat16)
    table_ref[...] = gate_table(ids_ref[...], gates_ref[...].astype(jnp.float32), rows)
    for n in range(width // TILE):
        columns = slice(n * TILE, (n + 1) * TILE)
        block = jnp.dot(h_ref[...], down_ref[:, columns], preferred_element_type=jnp.float32)
        out_ref[:, :, columns] = block.astype(jnp.bfloat16).reshape(experts, pair, TILE)


def combine_kernel(table_ref, rows_ref, out_ref):
    experts, pair, width = rows_ref.shape
    for n in range(width // TILE):
        columns = slice(n * TILE, (n + 1) * TILE)
        block = rows_ref[:, :, columns].reshape(experts * pair, TILE)
        total = jnp.dot(table_ref[...], block, preferred_element_type=jnp.float32)
        out_ref[:, columns] = total.astype(jnp.bfloat16)


def exchange(blocks):
    return lax.all_to_all(blocks, ("node", "local"), split_axis=0, concat_axis=0, tiled=True)


def local(tokens, expert_ids, gate_values, w_gate, w_up, w_down):
    tok_count, width = tokens.shape
    topk = expert_ids.shape[1]
    hid = w_gate.shape[2]
    experts = lax.axis_size("node") * lax.axis_size("local")
    rows = experts * PAIR
    bf16 = jnp.bfloat16
    hbm = pl.BlockSpec(memory_space=pltpu.HBM)
    vmem = pl.BlockSpec(memory_space=pltpu.VMEM)
    ids_t = expert_ids.T
    outgoing = pl.pallas_call(
        dispatch_kernel,
        out_shape=jax.ShapeDtypeStruct((experts, PAIR, width), bf16),
        in_specs=[hbm] * 2,
        out_specs=vmem,
        scratch_shapes=[
            pltpu.VMEM((topk, tok_count), jnp.int32),
            pltpu.VMEM((tok_count, width), bf16),
            pltpu.SemaphoreType.DMA((2,)),
        ],
        compiler_params=pltpu.CompilerParams(vmem_limit_bytes=12 * MIB),
        cost_estimate=pl.CostEstimate(
            flops=30_000_000_000, bytes_accessed=60_000_000, transcendentals=0
        ),
    )(*(pltpu.with_memory_space_constraint(v, pltpu.HBM) for v in (ids_t, tokens)))
    incoming = exchange(outgoing)
    result, table = pl.pallas_call(
        expert_kernel,
        out_shape=[
            jax.ShapeDtypeStruct((experts, PAIR, width), bf16),
            jax.ShapeDtypeStruct((tok_count, rows), bf16),
        ],
        in_specs=[vmem] * 6,
        out_specs=[vmem] * 2,
        scratch_shapes=[pltpu.VMEM((rows, width), bf16), pltpu.VMEM((rows, hid), bf16)],
        compiler_params=pltpu.CompilerParams(vmem_limit_bytes=20 * MIB),
        cost_estimate=pl.CostEstimate(
            flops=6 * rows * width * hid, bytes_accessed=6 * width * hid, transcendentals=rows * hid
        ),
    )(incoming, w_gate[0], w_up[0], w_down[0], ids_t, gate_values.T)
    answered = exchange(result)
    return pl.pallas_call(
        combine_kernel,
        out_shape=jax.ShapeDtypeStruct((tok_count, width), bf16),
        in_specs=[vmem] * 2,
        out_specs=vmem,
        compiler_params=pltpu.CompilerParams(vmem_limit_bytes=12 * MIB),
        cost_estimate=pl.CostEstimate(
            flops=2 * rows * tok_count * width, bytes_accessed=2 * rows * width, transcendentals=0
        ),
    )(table, answered)


def solution(mesh):
    return jax.shard_map(
        local,
        mesh=mesh,
        in_specs=(
            P(("node", "local"), None),
            P(("node", "local"), None),
            P(("node", "local"), None),
            P(("node", "local"), None, None),
            P(("node", "local"), None, None),
            P(("node", "local"), None, None),
        ),
        out_specs=P(("node", "local"), None),
        check_vma=False,
    )
```

```python
import jax
import jax.numpy as jnp
from jax import lax
from jax.experimental import pallas as pl
from jax.experimental.pallas import tpu as pltpu
from jax.sharding import PartitionSpec as P

PAIR = 2
TILE = 512
MIB = 1 << 20


CORES = 2


def expert_of(index, core, width):
    return (index // width) * (CORES * width) + core * width + (index & (width - 1))


def ranks(used):
    count = used.shape[1]
    column = lax.broadcasted_iota(jnp.int32, (count, count), 1)
    token = lax.broadcasted_iota(jnp.int32, (count, count), 0)
    weight = jnp.where(token < column, 1.0, jnp.where(token == column, -64.0, 0.0))
    rank = jnp.dot(used.astype(jnp.bfloat16), weight.astype(jnp.bfloat16), preferred_element_type=jnp.float32)
    return (rank + 64.0).astype(jnp.int32)


def dispatch_kernel(ids_ref, tokens_ref, out_ref):
    chips, block, width = out_ref.shape
    rows = chips * block
    tok_count = tokens_ref.shape[0]
    topk = ids_ref.shape[0] // CORES
    core = lax.axis_index("core")
    places = lax.axis_size("local")
    row = lax.broadcasted_iota(jnp.int32, (rows, tok_count), 0)
    column = lax.broadcasted_iota(jnp.int32, (rows, tok_count), 1)
    expert = jnp.where(
        ((row >> 1) & 1) == column // (tok_count // CORES), expert_of(row >> 2, core, places), -1
    )
    ids = jnp.concatenate([ids_ref[c * topk : (c + 1) * topk, :] for c in range(CORES)], axis=1)
    used = jnp.zeros((rows, tok_count), jnp.float32)
    for k in range(topk):
        used = jnp.where(ids[k : k + 1, :] == expert, 1.0, used)
    chosen = jnp.where(ranks(used) == (row & (PAIR - 1)), 1.0, 0.0).astype(jnp.bfloat16)
    for n in range(width // TILE):
        columns = slice(n * TILE, (n + 1) * TILE)
        total = jnp.dot(chosen, tokens_ref[:, columns], preferred_element_type=jnp.float32)
        out_ref[:, :, columns] = total.astype(jnp.bfloat16).reshape(chips, block, TILE)


def gate_table(ids_t, gates_t, rows):
    topk, tok_count = ids_t.shape
    row = lax.broadcasted_iota(jnp.int32, (rows, tok_count), 0)
    expert = expert_of(row >> 2, (row >> 1) & 1, lax.axis_size("local"))
    used = jnp.zeros((rows, tok_count), jnp.float32)
    gate = jnp.zeros((rows, tok_count), jnp.float32)
    for k in range(topk):
        hit = ids_t[k : k + 1, :] == expert
        used = jnp.where(hit, 1.0, used)
        gate = jnp.where(hit, gates_t[k : k + 1, :], gate)
    return jnp.where(ranks(used) == (row & (PAIR - 1)), gate, 0.0).T.astype(jnp.bfloat16)


def expert_kernel(rows_ref, gate_ref, up_ref, down_ref, ids_ref, gates_ref, out_ref, table_ref, x_ref, h_ref):
    experts, pair, width = out_ref.shape
    rows = experts * pair
    hid = gate_ref.shape[1]
    for n in range(width // TILE):
        columns = slice(n * TILE, (n + 1) * TILE)
        x_ref[:, columns] = rows_ref[:, :, columns].reshape(rows, TILE)
    for n in range(hid // TILE):
        columns = slice(n * TILE, (n + 1) * TILE)
        gate = jnp.dot(x_ref[...], gate_ref[:, columns], preferred_element_type=jnp.float32)
        upper = jnp.dot(x_ref[...], up_ref[:, columns], preferred_element_type=jnp.float32)
        h_ref[:, columns] = (gate / (1.0 + jnp.exp(-gate)) * upper).astype(jnp.bfloat16)
    table_ref[...] = gate_table(ids_ref[...], gates_ref[...].astype(jnp.float32), rows)
    for n in range(width // TILE):
        columns = slice(n * TILE, (n + 1) * TILE)
        block = jnp.dot(h_ref[...], down_ref[:, columns], preferred_element_type=jnp.float32)
        out_ref[:, :, columns] = block.astype(jnp.bfloat16).reshape(experts, pair, TILE)


def combine_kernel(table_ref, rows_ref, out_ref):
    experts, pair, width = rows_ref.shape
    for n in range(width // TILE):
        columns = slice(n * TILE, (n + 1) * TILE)
        block = rows_ref[:, :, columns].reshape(experts * pair, TILE)
        total = jnp.dot(table_ref[...], block, preferred_element_type=jnp.float32)
        out_ref[:, columns] = total.astype(jnp.bfloat16)


def exchange(blocks, axes):
    return lax.all_to_all(blocks, axes, split_axis=0, concat_axis=0, tiled=True)


def local(tokens, expert_ids, gate_values, w_gate, w_up, w_down):
    tok_count, width = tokens.shape
    hid = w_gate.shape[2]
    chips = lax.axis_size("z") * lax.axis_size("local")
    experts = chips * CORES
    rows = experts * PAIR
    bf16 = jnp.bfloat16
    vmem = pl.BlockSpec(memory_space=pltpu.VMEM)
    ids_t = expert_ids.T
    both_ids = lax.all_gather(ids_t, "core", axis=0, tiled=True)
    both_tokens = lax.all_gather(tokens, "core", axis=0, tiled=True)
    outgoing = pl.pallas_call(
        dispatch_kernel,
        out_shape=jax.ShapeDtypeStruct((chips, CORES * PAIR, width), bf16),
        in_specs=[vmem] * 2,
        out_specs=vmem,
        compiler_params=pltpu.CompilerParams(vmem_limit_bytes=12 * MIB),
        cost_estimate=pl.CostEstimate(
            flops=30_000_000_000, bytes_accessed=60_000_000, transcendentals=0
        ),
    )(both_ids, both_tokens)
    incoming = exchange(outgoing, ("z", "local"))
    result, table = pl.pallas_call(
        expert_kernel,
        out_shape=[
            jax.ShapeDtypeStruct((experts, PAIR, width), bf16),
            jax.ShapeDtypeStruct((tok_count, rows), bf16),
        ],
        in_specs=[vmem] * 6,
        out_specs=[vmem] * 2,
        scratch_shapes=[pltpu.VMEM((rows, width), bf16), pltpu.VMEM((rows, hid), bf16)],
        compiler_params=pltpu.CompilerParams(vmem_limit_bytes=20 * MIB),
        cost_estimate=pl.CostEstimate(
            flops=6 * rows * width * hid, bytes_accessed=6 * width * hid, transcendentals=rows * hid
        ),
    )(incoming, w_gate[0], w_up[0], w_down[0], ids_t, gate_values.T)
    answered = exchange(result, ("z", "local", "core"))
    return pl.pallas_call(
        combine_kernel,
        out_shape=jax.ShapeDtypeStruct((tok_count, width), bf16),
        in_specs=[vmem] * 2,
        out_specs=vmem,
        compiler_params=pltpu.CompilerParams(vmem_limit_bytes=12 * MIB),
        cost_estimate=pl.CostEstimate(
            flops=2 * rows * tok_count * width, bytes_accessed=2 * rows * width, transcendentals=0
        ),
    )(table, answered)


def solution(mesh):
    nodes, places = mesh.devices.shape
    devices = mesh.devices.reshape(nodes // CORES, CORES, places)
    axes = ("z", "core", "local")
    flat = P(axes, None)
    whole = P(axes, None, None)
    return jax.shard_map(
        local,
        mesh=jax.sharding.Mesh(devices, axes),
        in_specs=(flat, flat, flat, whole, whole, whole),
        out_specs=flat,
        check_vma=False,
    )
```

```python
import jax
import jax.numpy as jnp
from jax import lax
from jax.experimental import pallas as pl
from jax.experimental.pallas import tpu as pltpu
from jax.sharding import PartitionSpec as P

PAIR = 2
TILE = 512
MIB = 1 << 20


ORDER = ("x", "y", "z", "core")


def routing(ids_t, rows):
    topk, tok_count = ids_t.shape
    row = lax.broadcasted_iota(jnp.int32, (rows, tok_count), 0)
    expert, rest = jnp.zeros_like(row), row >> 1
    stride = {"x": 1, "y": lax.axis_size("x")}
    stride["core"] = stride["y"] * lax.axis_size("y")
    stride["z"] = stride["core"] * lax.axis_size("core")
    for axis in reversed(ORDER):
        size = lax.axis_size(axis)
        expert = expert + (rest & (size - 1)) * stride[axis]
        rest = rest >> (size.bit_length() - 1)
    used = jnp.zeros((rows, tok_count), jnp.float32)
    for k in range(topk):
        used = jnp.where(ids_t[k : k + 1, :] == expert, 1.0, used)
    column = lax.broadcasted_iota(jnp.int32, (tok_count, tok_count), 1)
    token = lax.broadcasted_iota(jnp.int32, (tok_count, tok_count), 0)
    weight = jnp.where(token < column, 1.0, jnp.where(token == column, -64.0, 0.0))
    rank = jnp.dot(used.astype(jnp.bfloat16), weight.astype(jnp.bfloat16), preferred_element_type=jnp.float32)
    return expert, (rank + 64.0).astype(jnp.int32) == (row & (PAIR - 1))


def dispatch_kernel(ids_hbm, tokens_hbm, out_ref, ids_ref, tokens_ref, sems):
    ids_copy = pltpu.make_async_copy(ids_hbm, ids_ref, sems.at[0])
    tokens_copy = pltpu.make_async_copy(tokens_hbm, tokens_ref, sems.at[1])
    ids_copy.start()
    tokens_copy.start()
    experts, pair, width = out_ref.shape
    ids_copy.wait()
    _, chosen = routing(ids_ref[...], experts * pair)
    chosen = jnp.where(chosen, 1.0, 0.0).astype(jnp.bfloat16)
    tokens_copy.wait()
    for n in range(width // TILE):
        columns = slice(n * TILE, (n + 1) * TILE)
        block = jnp.dot(chosen, tokens_ref[:, columns], preferred_element_type=jnp.float32)
        out_ref[:, :, columns] = block.astype(jnp.bfloat16).reshape(experts, pair, TILE)


def gate_table(ids_t, gates_t, rows):
    expert, chosen = routing(ids_t, rows)
    gate = jnp.zeros(expert.shape, jnp.float32)
    for k in range(ids_t.shape[0]):
        gate = jnp.where(ids_t[k : k + 1, :] == expert, gates_t[k : k + 1, :], gate)
    return jnp.where(chosen, gate, 0.0).T.astype(jnp.bfloat16)


def expert_kernel(rows_ref, gate_ref, up_ref, down_ref, ids_ref, gates_ref, out_ref, table_ref, x_ref, h_ref):
    experts, pair, width = rows_ref.shape
    rows = experts * pair
    hid = gate_ref.shape[1]
    for n in range(width // TILE):
        columns = slice(n * TILE, (n + 1) * TILE)
        x_ref[:, columns] = rows_ref[:, :, columns].reshape(rows, TILE)
    for n in range(hid // TILE):
        columns = slice(n * TILE, (n + 1) * TILE)
        gate = jnp.dot(x_ref[...], gate_ref[:, columns], preferred_element_type=jnp.float32)
        upper = jnp.dot(x_ref[...], up_ref[:, columns], preferred_element_type=jnp.float32)
        h_ref[:, columns] = (gate / (1.0 + jnp.exp(-gate)) * upper).astype(jnp.bfloat16)
    table_ref[...] = gate_table(ids_ref[...], gates_ref[...].astype(jnp.float32), rows)
    for n in range(width // TILE):
        columns = slice(n * TILE, (n + 1) * TILE)
        block = jnp.dot(h_ref[...], down_ref[:, columns], preferred_element_type=jnp.float32)
        out_ref[:, :, columns] = block.astype(jnp.bfloat16).reshape(experts, pair, TILE)


def combine_kernel(table_ref, rows_ref, out_ref):
    experts, pair, width = rows_ref.shape
    for n in range(width // TILE):
        columns = slice(n * TILE, (n + 1) * TILE)
        block = rows_ref[:, :, columns].reshape(experts * pair, TILE)
        total = jnp.dot(table_ref[...], block, preferred_element_type=jnp.float32)
        out_ref[:, columns] = total.astype(jnp.bfloat16)


def exchange(blocks):
    return lax.all_to_all(blocks, ORDER, split_axis=0, concat_axis=0, tiled=True)


def local(tokens, expert_ids, gate_values, w_gate, w_up, w_down):
    tok_count, width = tokens.shape
    topk = expert_ids.shape[1]
    hid = w_gate.shape[2]
    experts = lax.axis_size(ORDER)
    rows = experts * PAIR
    bf16 = jnp.bfloat16
    hbm = pl.BlockSpec(memory_space=pltpu.HBM)
    vmem = pl.BlockSpec(memory_space=pltpu.VMEM)
    ids_t = expert_ids.T
    outgoing = pl.pallas_call(
        dispatch_kernel,
        out_shape=jax.ShapeDtypeStruct((experts, PAIR, width), bf16),
        in_specs=[hbm] * 2,
        out_specs=vmem,
        scratch_shapes=[
            pltpu.VMEM((topk, tok_count), jnp.int32),
            pltpu.VMEM((tok_count, width), bf16),
            pltpu.SemaphoreType.DMA((2,)),
        ],
        compiler_params=pltpu.CompilerParams(vmem_limit_bytes=12 * MIB),
        cost_estimate=pl.CostEstimate(
            flops=30_000_000_000, bytes_accessed=60_000_000, transcendentals=0
        ),
    )(*(pltpu.with_memory_space_constraint(v, pltpu.HBM) for v in (ids_t, tokens)))
    incoming = exchange(outgoing)
    result, table = pl.pallas_call(
        expert_kernel,
        out_shape=[
            jax.ShapeDtypeStruct((experts, PAIR, width), bf16),
            jax.ShapeDtypeStruct((tok_count, rows), bf16),
        ],
        in_specs=[vmem] * 6,
        out_specs=[vmem] * 2,
        scratch_shapes=[pltpu.VMEM((rows, width), bf16), pltpu.VMEM((rows, hid), bf16)],
        compiler_params=pltpu.CompilerParams(vmem_limit_bytes=20 * MIB),
        cost_estimate=pl.CostEstimate(
            flops=6 * rows * width * hid, bytes_accessed=6 * width * hid, transcendentals=rows * hid
        ),
    )(incoming, w_gate[0], w_up[0], w_down[0], ids_t, gate_values.T)
    answered = exchange(result)
    return pl.pallas_call(
        combine_kernel,
        out_shape=jax.ShapeDtypeStruct((tok_count, width), bf16),
        in_specs=[vmem] * 2,
        out_specs=vmem,
        compiler_params=pltpu.CompilerParams(vmem_limit_bytes=12 * MIB),
        cost_estimate=pl.CostEstimate(
            flops=2 * rows * tok_count * width, bytes_accessed=2 * rows * width, transcendentals=0
        ),
    )(table, answered)


def solution(mesh):
    axes = ("z", "core", "y", "x")
    flat = P(axes, None)
    whole = P(axes, None, None)
    return jax.shard_map(
        local,
        mesh=jax.sharding.Mesh(mesh.devices.reshape(4, 2, 4, 4), axes),
        in_specs=(flat, flat, flat, whole, whole, whole),
        out_specs=flat,
        check_vma=False,
    )
```

```python
import jax
import jax.numpy as jnp
from jax import lax
from jax.experimental import pallas as pl
from jax.experimental.pallas import tpu as pltpu
from jax.sharding import PartitionSpec as P

PAIR = 2
TILE = 512
MIB = 1 << 20


def routing(ids_t, rows):
    topk, tok_count = ids_t.shape
    row = lax.broadcasted_iota(jnp.int32, (rows, tok_count), 0)
    expert = row >> 1
    used = jnp.zeros((rows, tok_count), jnp.float32)
    for k in range(topk):
        used = jnp.where(ids_t[k : k + 1, :] == expert, 1.0, used)
    column = lax.broadcasted_iota(jnp.int32, (tok_count, tok_count), 1)
    token = lax.broadcasted_iota(jnp.int32, (tok_count, tok_count), 0)
    weight = jnp.where(token < column, 1.0, jnp.where(token == column, -64.0, 0.0))
    rank = jnp.dot(used.astype(jnp.bfloat16), weight.astype(jnp.bfloat16), preferred_element_type=jnp.float32)
    return expert, (rank + 64.0).astype(jnp.int32) == (row & (PAIR - 1))


def dispatch_kernel(ids_hbm, tokens_hbm, out_ref, ids_ref, tokens_ref, sems):
    ids_copy = pltpu.make_async_copy(ids_hbm, ids_ref, sems.at[0])
    tokens_copy = pltpu.make_async_copy(tokens_hbm, tokens_ref, sems.at[1])
    ids_copy.start()
    tokens_copy.start()
    experts, pair, width = out_ref.shape
    ids_copy.wait()
    _, chosen = routing(ids_ref[...], experts * pair)
    chosen = jnp.where(chosen, 1.0, 0.0).astype(jnp.bfloat16)
    tokens_copy.wait()
    for n in range(width // TILE):
        columns = slice(n * TILE, (n + 1) * TILE)
        block = jnp.dot(chosen, tokens_ref[:, columns], preferred_element_type=jnp.float32)
        out_ref[:, :, columns] = block.astype(jnp.bfloat16).reshape(experts, pair, TILE)


def gate_table(ids_t, gates_t, rows):
    expert, chosen = routing(ids_t, rows)
    gate = jnp.zeros(expert.shape, jnp.float32)
    for k in range(ids_t.shape[0]):
        gate = jnp.where(ids_t[k : k + 1, :] == expert, gates_t[k : k + 1, :], gate)
    return jnp.where(chosen, gate, 0.0).T.astype(jnp.bfloat16)


def expert_kernel(rows_ref, gate_ref, up_ref, down_ref, ids_ref, gates_ref, out_ref, table_ref, x_ref, h_ref):
    experts, pair, width = rows_ref.shape
    rows = experts * pair
    hid = gate_ref.shape[1]
    table_ref[...] = gate_table(ids_ref[...], gates_ref[...].astype(jnp.float32), rows)
    for n in range(width // TILE):
        columns = slice(n * TILE, (n + 1) * TILE)
        x_ref[:, columns] = rows_ref[:, :, columns].reshape(rows, TILE)
    for n in range(hid // TILE):
        columns = slice(n * TILE, (n + 1) * TILE)
        gate = jnp.dot(x_ref[...], gate_ref[:, columns], preferred_element_type=jnp.float32)
        upper = jnp.dot(x_ref[...], up_ref[:, columns], preferred_element_type=jnp.float32)
        h_ref[:, columns] = (gate / (1.0 + jnp.exp(-gate)) * upper).astype(jnp.bfloat16)
    for n in range(width // TILE):
        columns = slice(n * TILE, (n + 1) * TILE)
        block = jnp.dot(h_ref[...], down_ref[:, columns], preferred_element_type=jnp.float32)
        out_ref[:, :, columns] = block.astype(jnp.bfloat16).reshape(experts, pair, TILE)


def combine_kernel(table_ref, rows_ref, out_ref):
    experts, pair, width = rows_ref.shape
    for n in range(width // TILE):
        columns = slice(n * TILE, (n + 1) * TILE)
        block = rows_ref[:, :, columns].reshape(experts * pair, TILE)
        total = jnp.dot(table_ref[...], block, preferred_element_type=jnp.float32)
        out_ref[:, columns] = total.astype(jnp.bfloat16)


def exchange(blocks):
    return lax.all_to_all(blocks, ("node", "local"), split_axis=0, concat_axis=0, tiled=True)


def local(tokens, expert_ids, gate_values, w_gate, w_up, w_down):
    tok_count, width = tokens.shape
    topk = expert_ids.shape[1]
    hid = w_gate.shape[2]
    experts = lax.axis_size("node") * lax.axis_size("local")
    rows = experts * PAIR
    bf16 = jnp.bfloat16
    hbm = pl.BlockSpec(memory_space=pltpu.HBM)
    vmem = pl.BlockSpec(memory_space=pltpu.VMEM)
    ids_t = expert_ids.T
    outgoing = pl.pallas_call(
        dispatch_kernel,
        out_shape=jax.ShapeDtypeStruct((experts, PAIR, width), bf16),
        in_specs=[hbm] * 2,
        out_specs=vmem,
        scratch_shapes=[
            pltpu.VMEM((topk, tok_count), jnp.int32),
            pltpu.VMEM((tok_count, width), bf16),
            pltpu.SemaphoreType.DMA((2,)),
        ],
        compiler_params=pltpu.CompilerParams(vmem_limit_bytes=12 * MIB),
        cost_estimate=pl.CostEstimate(
            flops=30_000_000_000, bytes_accessed=60_000_000, transcendentals=0
        ),
    )(*(pltpu.with_memory_space_constraint(v, pltpu.HBM) for v in (ids_t, tokens)))
    incoming = exchange(outgoing)
    result, table = pl.pallas_call(
        expert_kernel,
        out_shape=[
            jax.ShapeDtypeStruct((experts, PAIR, width), bf16),
            jax.ShapeDtypeStruct((tok_count, rows), bf16),
        ],
        in_specs=[vmem] * 6,
        out_specs=[vmem] * 2,
        scratch_shapes=[pltpu.VMEM((rows, width), bf16), pltpu.VMEM((rows, hid), bf16)],
        compiler_params=pltpu.CompilerParams(vmem_limit_bytes=20 * MIB),
        cost_estimate=pl.CostEstimate(
            flops=6 * rows * width * hid, bytes_accessed=6 * width * hid, transcendentals=rows * hid
        ),
    )(incoming, w_gate[0], w_up[0], w_down[0], ids_t, gate_values.T)
    answered = exchange(result)
    return pl.pallas_call(
        combine_kernel,
        out_shape=jax.ShapeDtypeStruct((tok_count, width), bf16),
        in_specs=[vmem] * 2,
        out_specs=vmem,
        compiler_params=pltpu.CompilerParams(vmem_limit_bytes=12 * MIB),
        cost_estimate=pl.CostEstimate(
            flops=2 * rows * tok_count * width, bytes_accessed=2 * rows * width, transcendentals=0
        ),
    )(table, answered)


def solution(mesh):
    return jax.shard_map(
        local,
        mesh=mesh,
        in_specs=(
            P(("node", "local"), None),
            P(("node", "local"), None),
            P(("node", "local"), None),
            P(("node", "local"), None, None),
            P(("node", "local"), None, None),
            P(("node", "local"), None, None),
        ),
        out_specs=P(("node", "local"), None),
        check_vma=False,
    )
```
